512 devices in a mesh: dp: 128 (over x, z, core), query: 4 (over y).
Axes of the slice: x: 4, y: 4, z: 16, core: 2. Of those that a mesh axis runs over, the one named last changes fastest.
Arguments:
- train_acts: bfloat16 [512, 64, 5120], P('dp'), may hold values from -45 to 45
- train_grads: bfloat16 [512, 64, 1280], P('dp'), may hold values from -6 to 6
- timestep: int32 [512], P('dp'), may hold values from 0 to 999
- time_weight: float32 [1000], replicated, may hold values from 0.5 to 2
- query_acts: bfloat16 [512, 64, 5120], P(('dp', 'query')), may hold values from -6 to 6
- query_grads: bfloat16 [512, 64, 1280], P(('dp', 'query')), may hold values from -6 to 6
- proj_in: bfloat16 [5120, 64], replicated, may hold values from -0.078125 to 0.078125
- proj_out: bfloat16 [1280, 64], replicated, may hold values from -0.15625 to 0.15625
- damping: float32 [1], replicated, may hold values from 0.5 to 2
Outputs:
- scores: float32 [512, 512], P(('dp', 'query'))
The draws below stay inside these ranges and needn't reach their ends.
All inputs are finite; a program needn't handle non-finite values.
Results may differ from the reference program's by a relative error of at most 0.0075.
Values may be sent and summed in bfloat16 or wider, within the bound.
A program may use at most 64 MiB of HBM per device.

```python
import math
import jax
import jax.numpy as jnp
from jax import lax

D_IN = 5120
D_OUT = 1280
R = 64
TOK = 64
NT = 1000
N_TRAIN = 512
NQ = 512


def draw_train_acts(key, part):
    key = jax.random.fold_in(key, 11)
    key_spread, key_base = jax.random.split(key)
    index = jnp.arange(N_TRAIN, dtype=jnp.float32)
    rise = jnp.exp(math.log(3.0) * index / max(N_TRAIN - 1, 1))
    spread = jnp.exp(jax.random.uniform(key_spread, (N_TRAIN,), jnp.float32, 0.0, math.log(3.0)))
    base = jnp.clip(jax.random.normal(key_base, (N_TRAIN, TOK, D_IN), jnp.float32), -5.0, 5.0)
    return (base * (rise * spread)[:, None, None]).astype(jnp.bfloat16)


def touch_ends(array, stream_key, least, top_value):
    spot = [jax.random.randint(jax.random.fold_in(stream_key, axis), (), 0, length) for axis, length in enumerate(array.shape)]
    main_axis = array.shape.index(max(array.shape))
    beside = spot[:main_axis] + [(spot[main_axis] + 1) % array.shape[main_axis]] + spot[main_axis + 1:]
    return array.at[tuple(spot)].set(least).at[tuple(beside)].set(top_value)


def levels(rng, dims, shards, low, high):
    def one(dim, parts):
        steps = jax.random.uniform(jax.random.fold_in(jax.random.fold_in(rng, 6), dim), (parts,), jnp.float32, low / len(shards), high / len(shards))
        return jnp.repeat(jnp.exp(steps), dims[dim] // parts).reshape((-1,) + (1,) * (len(dims) - dim - 1))

    loudness = one(*shards[0])
    for cut in shards[1:]:
        loudness = loudness * one(*cut)
    return loudness


def centred(own_key, shape, scale, bound, cuts=(), kind=jnp.bfloat16):
    array = jax.random.normal(own_key, shape, jnp.float32) * scale
    if len(cuts) > 0:
        array = levels(own_key, shape, cuts, -0.22, 0.18) * array
    return jnp.clip(array, min=-bound, max=bound).astype(kind)


def setup_inputs(seed: int = 0) -> dict:
    keys = jax.random.split(jax.random.key(seed), 10)
    return {
        "train_acts": draw_train_acts(jax.random.fold_in(keys[9], 71), 0),
        "train_grads": centred(keys[1], (N_TRAIN, TOK, D_OUT), 1.0, 6.0, ((0, 128),)),
        "timestep": touch_ends(jax.random.randint(keys[2], (N_TRAIN,), 0, NT), jax.random.fold_in(keys[2], 1), 0, NT - 1).astype(jnp.int32),
        "time_weight": jnp.clip(jnp.exp(jax.random.uniform(keys[3], (NT,), jnp.float32, math.log(0.5), math.log(2.0))), 0.5, 2.0),
        "query_acts": centred(keys[4], (NQ, TOK, D_IN), 1.0, 6.0, ((0, 512),)),
        "query_grads": centred(keys[5], (NQ, TOK, D_OUT), 1.0, 6.0, ((0, 512),)),
        "proj_in": centred(keys[6], (D_IN, R), D_IN ** -0.5, 0.078125),
        "proj_out": centred(keys[7], (D_OUT, R), D_OUT ** -0.5, 0.15625),
        "damping": jnp.clip(jnp.exp(jax.random.uniform(keys[8], (1,), jnp.float32, math.log(0.5), math.log(2.0))), 0.5, 2.0),
    }


def project(acts, grads, proj_in, proj_out):
    count, tok, width_in = acts.shape
    width_out = grads.shape[2]
    act_proj = jnp.dot(acts.reshape(count * tok, width_in).astype(jnp.float32), proj_in.astype(jnp.float32), preferred_element_type=jnp.float32).astype(jnp.bfloat16)
    grad_proj = jnp.dot(grads.reshape(count * tok, width_out).astype(jnp.float32), proj_out.astype(jnp.float32), preferred_element_type=jnp.float32).astype(jnp.bfloat16)
    act_proj = act_proj.reshape(count, tok, -1).astype(jnp.float32)
    grad_proj = grad_proj.reshape(count, tok, -1).astype(jnp.float32)
    return jnp.einsum('etr,ets->ers', grad_proj, act_proj)

def reference(train_acts, train_grads, timestep, time_weight, query_acts, query_grads, proj_in, proj_out, damping):
    outer = project(train_acts, train_grads, proj_in, proj_out)
    onehot = (timestep[:, None] == jnp.arange(NT, dtype=jnp.int32)[None, :]).astype(jnp.float32)
    weights = jnp.sum(onehot * time_weight[None, :], axis=1)
    train_vec = (outer * weights[:, None, None]).reshape(N_TRAIN, R * R).astype(jnp.bfloat16)
    query_vec = project(query_acts, query_grads, proj_in, proj_out).reshape(NQ, R * R).astype(jnp.bfloat16)
    kernel = lax.dot_general(train_vec.astype(jnp.float32), train_vec.astype(jnp.float32), (((1,), (1,)), ((), ())), preferred_element_type=jnp.float32)
    trace = jnp.sum(train_vec.astype(jnp.float32) ** 2)
    lam = damping[0] * trace / (R * R)
    matrix = kernel + lam * jnp.eye(N_TRAIN, dtype=jnp.float32)
    cross = lax.dot_general(query_vec.astype(jnp.float32), train_vec.astype(jnp.float32), (((1,), (1,)), ((), ())), preferred_element_type=jnp.float32)
    factor = jnp.linalg.cholesky(matrix)
    solved = jax.scipy.linalg.cho_solve((factor, True), cross.T)
    return solved.T
```

```python
import functools

import jax
import jax.numpy as jnp
from jax import lax
from jax.experimental import pallas as pl
from jax.experimental.pallas import tpu as pltpu
from jax.sharding import PartitionSpec as P

MESH = pl.DeviceIdType.MESH
BF = jnp.bfloat16
F32 = jnp.float32

NX, NZ, NC, NY = 4, 16, 2, 4
NB, NA = 4, 4
TOL = 2e-5
MAX_STEPS = 4096


def dot(a, b, dims):
    return lax.dot_general(a, b, (dims, ((), ())), preferred_element_type=F32)


def pair_tiles(m):
    return jnp.concatenate([m[:32], m[32:]], axis=1)


def gram_kernel(
    tacts_hbm, tgrads_hbm, step_ref, weight_ref, qacts_hbm, qgrads_hbm, pin_hbm, pout_hbm,
    gram_ref, cross_ref,
    tacts, tgrads, qacts, qgrads, pin, pout,
    wide, sendbuf, landing, wide2, spread, query_rows, table,
    load_sem, a_send, a_recv, b_send, b_recv, c_send, c_recv, s_send, s_recv,
):
    dp = lax.axis_index("dp")
    y = lax.axis_index("query")
    x = dp // (NZ * NC)
    z = lax.rem(dp // NC, NZ)
    c = lax.rem(dp, NC)
    a = lax.rem(z, NA)
    b = z // NA

    def device(dx=0, dz=0, dc=0, dy=0):
        x1 = lax.rem(x + (dx + NX), NX)
        z1 = lax.rem(z + (dz + NZ), NZ)
        c1 = lax.rem(c + dc, NC)
        y1 = lax.rem(y + (dy + NY), NY)
        return ((x1 * NZ + z1) * NC + c1, y1)

    loads = []
    for i, (src, dst) in enumerate(
        [(pin_hbm, pin), (pout_hbm, pout), (tacts_hbm, tacts), (tgrads_hbm, tgrads),
         (qacts_hbm, qacts), (qgrads_hbm, qgrads)]
    ):
        copy = pltpu.make_async_copy(src, dst, load_sem.at[i])
        copy.start()
        loads.append(copy)

    barrier = pltpu.get_barrier_semaphore()
    line = [
        (dj, dx, dc)
        for dj in range(NB) for dx in range(NX) for dc in range(NC)
        if (dj, dx, dc) != (0, 0, 0)
    ]
    partners = [device(dz=NA * dj, dx=dx, dc=dc) for dj, dx, dc in line]
    partners += [device(dz=d) for d in (1, -1, 2, -2)]
    partners += [device(dy=d) for d in (1, 2, 3)]
    for partner in partners:
        pl.semaphore_signal(barrier, inc=1, device_id=partner, device_id_type=MESH)

    for i in range(4):
        loads[i].wait()
    count, tok, width_in = tacts.shape
    width_out = tgrads.shape[2]
    grad_proj = dot(tgrads[...].reshape(count * tok, width_out), pout[...], ((1,), (0,))).astype(BF)
    act_proj = dot(tacts[...].reshape(count * tok, width_in), pin[...], ((1,), (0,))).astype(BF)
    for e in range(count):
        rows = slice(e * tok, (e + 1) * tok)
        outer = dot(grad_proj[rows], act_proj[rows], ((0,), (0,)))
        weight = weight_ref[step_ref[e]]
        wide[pl.ds(e, 32, stride=4), :] = pair_tiles(outer * weight)

    def tile_for(x1, c1):
        left = wide[pl.ds(pl.multiple_of(8 * (2 * x1 + c1), 8), 8), :]
        right = wide[pl.ds(pl.multiple_of(64 + 8 * (2 * y + c1), 8), 8), :]
        return jnp.concatenate([left, right], axis=0).astype(BF)

    for x1 in range(NX):
        for c1 in range(NC):
            sendbuf[2 * x1 + c1] = tile_for(x1, c1)
    me = 2 * x + c
    landing[b, me] = tile_for(x, c)

    pl.semaphore_wait(barrier, len(partners))

    sends = []
    for dj, dx, dc in line:
        x1 = lax.rem(x + dx, NX)
        c1 = lax.rem(c + dc, NC)
        copy = pltpu.make_async_remote_copy(
            src_ref=sendbuf.at[2 * x1 + c1], dst_ref=landing.at[b, me],
            send_sem=a_send.at[dj, dx, dc], recv_sem=a_recv.at[dj, dx, dc],
            device_id=device(dz=NA * dj, dx=dx, dc=dc), device_id_type=MESH,
        )
        copy.start()
        sends.append(copy)

    loads[4].wait()
    loads[5].wait()
    qg = dot(qgrads[0], pout[...], ((1,), (0,))).astype(BF)
    qa = dot(qacts[0], pin[...], ((1,), (0,))).astype(BF)
    query = pair_tiles(dot(qg, qa, ((0,), (0,))))
    for k in range(16):
        row = jnp.concatenate([query[2 * k:2 * k + 1], query[2 * k + 1:2 * k + 2]], axis=1)
        query_rows[k] = jnp.broadcast_to(row, (16, 256)).astype(BF)

    for dj, dx, dc in line:
        b1 = lax.rem(b + (NB - dj), NB)
        src = 2 * lax.rem(x + (NX - dx), NX) + lax.rem(c + dc, NC)
        pltpu.make_async_remote_copy(
            src_ref=sendbuf.at[0], dst_ref=landing.at[b1, src],
            send_sem=a_send.at[dj, dx, dc], recv_sem=a_recv.at[dj, dx, dc],
            device_id=device(dz=-NA * dj, dx=-dx, dc=dc), device_id_type=MESH,
        ).wait_recv()

    kx = 2 * x + c
    ky = 8 + 2 * y + c
    for b1 in range(NB):
        wide2[...] = landing[b1].astype(F32).reshape(128, 128)
        for t in range(4):
            for e in range(4):
                spread[t, pl.ds(e, 8, stride=4), :] = wide2[pl.ds(4 * t + e, 8, stride=16), :]
        table[kx, b1, a] = jnp.concatenate([spread[0], spread[1]], axis=1).astype(BF)
        table[ky, b1, a] = jnp.concatenate([spread[2], spread[3]], axis=1).astype(BF)

    def class_of(j):
        return lax.rem(a + (0, NA - 1, 1, 2)[j], NA)

    def move(k, j, send_sem, recv_sem, target):
        part = table.at[k, :, class_of(j)]
        return pltpu.make_async_remote_copy(
            src_ref=part, dst_ref=part, send_sem=send_sem, recv_sem=recv_sem,
            device_id=target, device_id_type=MESH,
        )

    for i, d in enumerate((1, -1, 2)):
        for kind, k in ((0, kx), (1, ky)):
            d1 = -d if (i == 2 and kind == 1) else d
            part = table.at[k, :, a]
            copy = pltpu.make_async_remote_copy(
                src_ref=part, dst_ref=part, send_sem=b_send.at[i, kind],
                recv_sem=b_recv.at[i, kind], device_id=device(dz=d1), device_id_type=MESH,
            )
            copy.start()
            sends.append(copy)

    sib = device(dc=1)

    def start(copy):
        copy.start()
        sends.append(copy)

    def fan_out(j):
        for d in (1, 3, 2):
            start(move(kx, j, c_send.at[j, 0, d], c_recv.at[j, 0, d], device(dx=d)))
            start(move(ky, j, c_send.at[j, 1, d], c_recv.at[j, 1, d], device(dy=d)))
        start(move(kx, j, s_send.at[j, 0, 0], s_recv.at[j, 0, 0], sib))
        start(move(ky, j, s_send.at[j, 1, 0], s_recv.at[j, 1, 0], sib))

    def pass_on(j):
        for d in (1, 3, 2):
            k = 2 * lax.rem(x + (NX - d), NX) + c
            move(k, j, c_send.at[j, 0, d], c_recv.at[j, 0, d], sib).wait_recv()
            start(move(k, j, s_send.at[j, 0, d], s_recv.at[j, 0, d], sib))
            k = 8 + 2 * lax.rem(y + (NY - d), NY) + c
            move(k, j, c_send.at[j, 1, d], c_recv.at[j, 1, d], sib).wait_recv()
            start(move(k, j, s_send.at[j, 1, d], s_recv.at[j, 1, d], sib))

    fan_out(0)
    for j in (1, 2, 3):
        for kind, k in ((0, kx), (1, ky)):
            move(k, j, b_send.at[j - 1, kind], b_recv.at[j - 1, kind], sib).wait_recv()
        fan_out(j)
    for j in range(4):
        pass_on(j)
    for j in range(4):
        for d in range(4):
            k = 2 * lax.rem(x + (NX - d), NX) + (1 - c)
            move(k, j, s_send.at[j, 0, d], s_recv.at[j, 0, d], sib).wait_recv()
            k = 8 + 2 * lax.rem(y + (NY - d), NY) + (1 - c)
            move(k, j, s_send.at[j, 1, d], s_recv.at[j, 1, d], sib).wait_recv()

    gram_ref[...] = jnp.zeros_like(gram_ref)
    cross_ref[...] = jnp.zeros_like(cross_ref)

    def accumulate(i, carry):
        rows = jnp.concatenate(
            [table[4 * i + k].reshape(512, 256) for k in range(4)], axis=1
        )
        queries = jnp.concatenate([query_rows[4 * i + k] for k in range(4)], axis=1)
        product = dot(jnp.concatenate([rows, queries], axis=0), rows, ((1,), (1,)))
        gram_ref[...] += product[:512]
        cross_ref[...] += product[512:520]
        return carry

    lax.fori_loop(0, 4, accumulate, 0)

    for copy in sends:
        copy.wait_send()


def solve_kernel(gram_ref, cross_ref, damping_ref, out_ref, column):
    rank2 = 4096.0
    eye = (
        lax.broadcasted_iota(jnp.int32, (128, 128), 0)
        == lax.broadcasted_iota(jnp.int32, (128, 128), 1)
    )
    diagonal = jnp.concatenate(
        [
            jnp.sum(
                jnp.where(eye, gram_ref[128 * t:128 * t + 128, 128 * t:128 * t + 128], 0.0),
                axis=0, keepdims=True,
            )
            for t in range(4)
        ],
        axis=1,
    )

    def total(v):
        return jnp.sum(v, axis=1, keepdims=True)

    lam = damping_ref[0] * total(diagonal) / rank2
    top = jnp.max(diagonal, axis=1, keepdims=True) + lam
    scale = 1.0 / top
    lam_scaled = lam * scale
    jacobi = 1.0 / (diagonal * scale + lam_scaled)
    size = jnp.max(jnp.abs(cross_ref[0:1]), axis=1, keepdims=True)
    size = jnp.where(size > 0.0, size, 1.0)
    bound = (TOL * lam_scaled) * (TOL * lam_scaled)

    def product(p):
        parts = [jnp.zeros((8, 128), F32) for _ in range(4)]
        for t in range(4):
            chunk = p[:, 128 * t:128 * t + 128]
            spread = jnp.broadcast_to(chunk, (128, 128)).T
            for u in range(4):
                tile = gram_ref[128 * t:128 * t + 128, 128 * u:128 * u + 128] * spread
                parts[u] += jnp.sum(tile.reshape(16, 8, 128), axis=0)
        whole = jnp.concatenate([jnp.sum(v, axis=0, keepdims=True) for v in parts], axis=1)
        return whole * scale + lam_scaled * p

    def go_on(state):
        step, more = state[0], state[1]
        return jnp.logical_and(step < MAX_STEPS, more)

    def advance(state):
        step, _, s, r, p, rz = state
        q = product(p)
        alpha = rz / total(p * q)
        s = s + alpha * p
        r = r - alpha * q
        u = r * jacobi
        rz_new = total(r * u)
        p = u + (rz_new / rz) * p
        more = (total(r * r) - bound * total(s * s))[0, 0] > 0.0
        return step + 1, more, s, r, p, rz_new

    r = cross_ref[0:1] / size
    u = r * jacobi
    rz = total(r * u)
    more = rz[0, 0] > 0.0
    state = (jnp.int32(0), more, jnp.zeros_like(r), r, u, rz)
    s = lax.while_loop(go_on, advance, state)[2] * (size * scale)

    for t in range(4):
        column[128 * t:128 * t + 128, :] = jnp.broadcast_to(s[:, 128 * t:128 * t + 128], (128, 128)).T
    for x in range(NX):
        rows = jnp.concatenate(
            [column[32 * z + 8 * x:32 * z + 8 * x + 8, :] for z in range(NZ)], axis=0
        )
        out_ref[:, 128 * x:128 * x + 128] = rows.T[0:1, :]


def body(
    train_acts, train_grads, timestep, time_weight, query_acts, query_grads, proj_in, proj_out,
    damping,
):
    any_spec = pl.BlockSpec(memory_space=pl.ANY)
    smem = pl.BlockSpec(memory_space=pltpu.SMEM)
    vmem = pl.BlockSpec(memory_space=pltpu.VMEM)
    dma = pltpu.SemaphoreType.DMA
    gram, cross = pl.pallas_call(
        gram_kernel,
        out_shape=(
            jax.ShapeDtypeStruct((512, 512), F32),
            jax.ShapeDtypeStruct((8, 512), F32),
        ),
        in_specs=[any_spec, any_spec, smem, smem, any_spec, any_spec, any_spec, any_spec],
        out_specs=(vmem, vmem),
        scratch_shapes=[
            pltpu.VMEM(train_acts.shape, BF),
            pltpu.VMEM(train_grads.shape, BF),
            pltpu.VMEM(query_acts.shape, BF),
            pltpu.VMEM(query_grads.shape, BF),
            pltpu.VMEM(proj_in.shape, BF),
            pltpu.VMEM(proj_out.shape, BF),
            pltpu.VMEM((128, 128), F32),
            pltpu.VMEM((8, 16, 128), BF),
            pltpu.VMEM((NB, 8, 16, 128), BF),
            pltpu.VMEM((128, 128), F32),
            pltpu.VMEM((4, 32, 128), F32),
            pltpu.VMEM((16, 16, 256), BF),
            pltpu.VMEM((16, NB, NA, 32, 256), BF),
            dma((6,)),
            dma((NB, NX, NC)),
            dma((NB, NX, NC)),
            dma((3, 2)),
            dma((3, 2)),
            dma((4, 2, 4)),
            dma((4, 2, 4)),
            dma((4, 2, 4)),
            dma((4, 2, 4)),
        ],
        compiler_params=pltpu.CompilerParams(
            collective_id=0, has_side_effects=True, vmem_limit_bytes=40 << 20
        ),
        name="gather_gram",
    )(train_acts, train_grads, timestep, time_weight, query_acts, query_grads, proj_in, proj_out)
    return pl.pallas_call(
        solve_kernel,
        out_shape=jax.ShapeDtypeStruct((1, 512), F32),
        in_specs=[vmem, vmem, smem],
        out_specs=vmem,
        scratch_shapes=[pltpu.VMEM((512, 128), F32)],
        compiler_params=pltpu.CompilerParams(vmem_limit_bytes=16 << 20),
        name="solve",
    )(gram, cross, damping)


def solution(mesh):
    return jax.shard_map(
        body,
        mesh=mesh,
        in_specs=(
            P("dp", None, None),
            P("dp", None, None),
            P("dp"),
            P(),
            P(("dp", "query"), None, None),
            P(("dp", "query"), None, None),
            P(),
            P(),
            P(),
        ),
        out_specs=P(("dp", "query"), None),
        check_vma=False,
    )
```

```python
import functools

import jax
import jax.numpy as jnp
from jax import lax
from jax.experimental import pallas as pl
from jax.experimental.pallas import tpu as pltpu
from jax.sharding import PartitionSpec as P

MESH = pl.DeviceIdType.MESH
BF = jnp.bfloat16
F32 = jnp.float32

NX, NZ, NC, NY = 4, 16, 2, 4
FAR = (0, 5, -5)
NEAR = {1: (1, 0), -1: (-1, 0), 2: (2, 0), -2: (-2, 0), 6: (1, 5), 4: (-1, 5), -6: (-1, -5),
        -4: (1, -5), 7: (2, 5), 3: (-2, 5), -7: (-2, -5), -3: (2, -5)}
LAST = ((3, 5), (-3, -5))
LAG = 13
TOL = 2e-5
MAX_STEPS = 4096


def dot(a, b, dims):
    return lax.dot_general(a, b, (dims, ((), ())), preferred_element_type=F32)


def pair_tiles(m):
    return jnp.concatenate([m[:32], m[32:]], axis=1)


def gram_kernel(
    tacts_hbm, tgrads_hbm, step_hbm, weight_hbm, qacts_hbm, qgrads_hbm, pin_hbm, pout_hbm,
    gram_ref, cross_ref,
    tacts, tgrads, qacts, qgrads, pin, pout, step_ref, weight_ref,
    wide, sendbuf, landing, wide2, spread, query_rows, table,
    load_sem, a_send, a_recv, b_send, b_recv, c_send, c_recv, s_send, s_recv,
):
    dp = lax.axis_index("dp")
    y = lax.axis_index("query")
    x = dp // (NZ * NC)
    z = lax.rem(dp // NC, NZ)
    c = lax.rem(dp, NC)

    def device(dx=0, dz=0, dc=0, dy=0):
        x1 = lax.rem(x + (dx + NX), NX)
        z1 = lax.rem(z + (dz + NZ), NZ)
        c1 = lax.rem(c + dc, NC)
        y1 = lax.rem(y + (dy + NY), NY)
        return ((x1 * NZ + z1) * NC + c1, y1)

    loads = []
    for i, (src, dst) in enumerate(
        [(step_hbm, step_ref), (weight_hbm, weight_ref), (pout_hbm, pout), (tgrads_hbm, tgrads),
         (pin_hbm, pin), (tacts_hbm, tacts), (qgrads_hbm, qgrads), (qacts_hbm, qacts)]
    ):
        copy = pltpu.make_async_copy(src, dst, load_sem.at[i])
        copy.start()
        loads.append(copy)

    barrier = pltpu.get_barrier_semaphore()
    line = [
        (i, dx, dc)
        for i in range(len(FAR)) for dx in range(NX) for dc in range(NC)
        if (i, dx, dc) != (0, 0, 0)
    ]
    partners = [device(dz=FAR[i], dx=dx, dc=dc) for i, dx, dc in line]
    partners += [device(dz=d) for d in (1, -1, 2, -2, 3, -3)]
    partners += [device(dy=d) for d in (1, 2, 3)]
    for partner in partners:
        pl.semaphore_signal(barrier, inc=1, device_id=partner, device_id_type=MESH)

    for i in range(6):
        loads[i].wait()
    count, tok, width_in = tacts.shape
    width_out = tgrads.shape[2]
    grad_proj = dot(tgrads[...].reshape(count * tok, width_out), pout[...], ((1,), (1,))).astype(BF)
    act_proj = dot(tacts[...].reshape(count * tok, width_in), pin[...], ((1,), (1,))).astype(BF)
    for e in range(count):
        rows = slice(e * tok, (e + 1) * tok)
        outer = dot(grad_proj[rows], act_proj[rows], ((0,), (0,)))
        weight = weight_ref[step_ref[e]]
        wide[pl.ds(e, 32, stride=4), :] = pair_tiles(outer * weight)

    def tile_for(x1, c1):
        left = wide[pl.ds(pl.multiple_of(8 * (2 * x1 + c1), 8), 8), :]
        right = wide[pl.ds(pl.multiple_of(64 + 8 * (2 * y + c1), 8), 8), :]
        return jnp.concatenate([left, right], axis=0).astype(BF)

    for x1 in range(NX):
        for c1 in range(NC):
            sendbuf[2 * x1 + c1] = tile_for(x1, c1)
    me = 2 * x + c
    landing[me] = tile_for(x, c)

    pl.semaphore_wait(barrier, len(partners))

    for i, dx, dc in line:
        x1 = lax.rem(x + dx, NX)
        c1 = lax.rem(c + dc, NC)
        pltpu.make_async_remote_copy(
            src_ref=sendbuf.at[2 * x1 + c1], dst_ref=landing.at[8 * i + me],
            send_sem=a_send, recv_sem=a_recv.at[i, dx, dc],
            device_id=device(dz=-FAR[i], dx=dx, dc=dc), device_id_type=MESH,
        ).start()

    loads[6].wait()
    loads[7].wait()
    qg = dot(qgrads[0], pout[...], ((1,), (1,))).astype(BF)
    qa = dot(qacts[0], pin[...], ((1,), (1,))).astype(BF)
    query = pair_tiles(dot(qg, qa, ((0,), (0,))))
    for k in range(16):
        row = jnp.concatenate([query[2 * k:2 * k + 1], query[2 * k + 1:2 * k + 2]], axis=1)
        query_rows[k] = jnp.broadcast_to(row, (16, 256)).astype(BF)

    kx = 2 * x + c
    ky = 8 + 2 * y + c
    sib = device(dc=1)

    def plane(o):
        return lax.rem(z + (o + NZ), NZ)

    def take(i):
        for i1, dx, dc in line:
            if i1 == i:
                src = 2 * lax.rem(x + (NX - dx), NX) + lax.rem(c + dc, NC)
                pltpu.make_async_remote_copy(
                    src_ref=sendbuf.at[0], dst_ref=landing.at[8 * i + src],
                    send_sem=a_send, recv_sem=a_recv.at[i, dx, dc],
                    device_id=sib, device_id_type=MESH,
                ).wait_recv()
        wide2[...] = landing[8 * i:8 * i + 8].astype(F32).reshape(128, 128)
        for t in range(4):
            for e in range(4):
                spread[t, pl.ds(e, 8, stride=4), :] = wide2[pl.ds(4 * t + e, 8, stride=16), :]
        o = plane(FAR[i])
        table[kx, o] = jnp.concatenate([spread[0], spread[1]], axis=1).astype(BF)
        table[ky, o] = jnp.concatenate([spread[2], spread[3]], axis=1).astype(BF)

    def move(k, o, send_sem, recv_sem, target):
        part = table.at[k, plane(o)]
        return pltpu.make_async_remote_copy(
            src_ref=part, dst_ref=part, send_sem=send_sem, recv_sem=recv_sem,
            device_id=target, device_id_type=MESH,
        )

    def relay(s):
        for o, (n, s1) in NEAR.items():
            if s1 == s:
                move(kx, s, b_send, b_recv.at[o + 7, 0], device(dz=-n)).start()
                move(ky, s, b_send, b_recv.at[o + 7, 1], device(dz=-n)).start()
        for kind, k in ((0, kx), (1, ky)):
            if LAST[kind][1] == s:
                move(k, s, b_send, b_recv.at[15, kind], device(dz=-LAST[kind][0])).start()

    def relayed(o):
        move(kx, o, b_send, b_recv.at[o + 7, 0], sib).wait_recv()
        move(ky, o, b_send, b_recv.at[o + 7, 1], sib).wait_recv()

    def fan_out(o):
        for d in (1, 3, 2):
            move(kx, o, c_send, c_recv.at[o + 7, 0, d], device(dx=d)).start()
            move(ky, o, c_send, c_recv.at[o + 7, 1, d], device(dy=d)).start()
        move(kx, o, s_send, s_recv, sib).start()
        move(ky, o, s_send, s_recv, sib).start()

    def pass_on(o):
        for d in (1, 3, 2):
            k = 2 * lax.rem(x + (NX - d), NX) + c
            move(k, o, c_send, c_recv.at[o + 7, 0, d], sib).wait_recv()
            move(k, o, s_send, s_recv, sib).start()
            k = 8 + 2 * lax.rem(y + (NY - d), NY) + c
            move(k, o, c_send, c_recv.at[o + 7, 1, d], sib).wait_recv()
            move(k, o, s_send, s_recv, sib).start()

    for i, s in enumerate(FAR):
        take(i)
        relay(s)
        fan_out(s)
    order = (*FAR, *NEAR, 8)
    passed = 0
    for done, o in enumerate((*NEAR, 8), len(FAR) + 1):
        relayed(o)
        fan_out(o)
        while passed < done - LAG:
            pass_on(order[passed])
            passed += 1
    for o in order[passed:]:
        pass_on(o)

    def drain(part, sem):
        pltpu.make_async_copy(part, part, sem).wait()

    drain(table.at[0:8], s_recv)

    gram_ref[...] = jnp.zeros_like(gram_ref)
    cross_ref[...] = jnp.zeros_like(cross_ref)

    def accumulate(i, carry):
        rows = jnp.concatenate(
            [table[4 * i + k].reshape(512, 256) for k in range(4)], axis=1
        )
        queries = jnp.concatenate([query_rows[4 * i + k] for k in range(4)], axis=1)
        product = dot(jnp.concatenate([rows, queries], axis=0), rows, ((1,), (1,)))
        gram_ref[...] += product[:512]
        cross_ref[...] += product[512:520]
        return carry

    lax.fori_loop(0, 4, accumulate, 0)

    drain(landing.at[0:len(line)], a_send)
    drain(table.at[0:2, 0:len(NEAR) + 1], b_send)
    drain(table.at[0:6], c_send)
    drain(table.at[0:8], s_send)


def solve_kernel(gram_ref, cross_ref, damping_ref, out_ref, column):
    rank2 = 4096.0
    eye = (
        lax.broadcasted_iota(jnp.int32, (128, 128), 0)
        == lax.broadcasted_iota(jnp.int32, (128, 128), 1)
    )
    diagonal = jnp.concatenate(
        [
            jnp.sum(
                jnp.where(eye, gram_ref[128 * t:128 * t + 128, 128 * t:128 * t + 128], 0.0),
                axis=0, keepdims=True,
            )
            for t in range(4)
        ],
        axis=1,
    )

    def total(v):
        return jnp.sum(v, axis=1, keepdims=True)

    lam = damping_ref[0] * total(diagonal) / rank2
    top = jnp.max(diagonal, axis=1, keepdims=True) + lam
    scale = 1.0 / top
    lam_scaled = lam * scale
    jacobi = 1.0 / (diagonal * scale + lam_scaled)
    size = jnp.max(jnp.abs(cross_ref[0:1]), axis=1, keepdims=True)
    size = jnp.where(size > 0.0, size, 1.0)
    bound = (TOL * lam_scaled) * (TOL * lam_scaled)

    def product(p):
        parts = [jnp.zeros((8, 128), F32) for _ in range(4)]
        for t in range(4):
            chunk = p[:, 128 * t:128 * t + 128]
            spread = jnp.broadcast_to(chunk, (128, 128)).T
            for u in range(4):
                tile = gram_ref[128 * t:128 * t + 128, 128 * u:128 * u + 128] * spread
                parts[u] += jnp.sum(tile.reshape(16, 8, 128), axis=0)
        whole = jnp.concatenate([jnp.sum(v, axis=0, keepdims=True) for v in parts], axis=1)
        return whole * scale + lam_scaled * p

    def go_on(state):
        step, more = state[0], state[1]
        return jnp.logical_and(step < MAX_STEPS, more)

    def advance(state):
        step, _, s, r, p, rz = state
        q = product(p)
        alpha = rz / total(p * q)
        s = s + alpha * p
        r = r - alpha * q
        u = r * jacobi
        rz_new = total(r * u)
        p = u + (rz_new / rz) * p
        more = (total(r * r) - bound * total(s * s))[0, 0] > 0.0
        return step + 1, more, s, r, p, rz_new

    r = cross_ref[0:1] / size
    u = r * jacobi
    rz = total(r * u)
    more = rz[0, 0] > 0.0
    state = (jnp.int32(0), more, jnp.zeros_like(r), r, u, rz)
    s = lax.while_loop(go_on, advance, state)[2] * (size * scale)

    for t in range(4):
        column[128 * t:128 * t + 128, :] = jnp.broadcast_to(s[:, 128 * t:128 * t + 128], (128, 128)).T
    for x in range(NX):
        rows = jnp.concatenate(
            [column[32 * z + 8 * x:32 * z + 8 * x + 8, :] for z in range(NZ)], axis=0
        )
        out_ref[:, 128 * x:128 * x + 128] = rows.T[0:1, :]


def body(
    train_acts, train_grads, timestep, time_weight, query_acts, query_grads, proj_in, proj_out,
    damping,
):
    any_spec = pl.BlockSpec(memory_space=pl.ANY)
    smem = pl.BlockSpec(memory_space=pltpu.SMEM)
    vmem = pl.BlockSpec(memory_space=pltpu.VMEM)
    dma = pltpu.SemaphoreType.DMA
    gram, cross = pl.pallas_call(
        gram_kernel,
        out_shape=(
            jax.ShapeDtypeStruct((512, 512), F32),
            jax.ShapeDtypeStruct((8, 512), F32),
        ),
        in_specs=[any_spec] * 8,
        out_specs=(vmem, vmem),
        scratch_shapes=[
            pltpu.VMEM(train_acts.shape, BF),
            pltpu.VMEM(train_grads.shape, BF),
            pltpu.VMEM(query_acts.shape, BF),
            pltpu.VMEM(query_grads.shape, BF),
            pltpu.VMEM(proj_in.shape[::-1], BF),
            pltpu.VMEM(proj_out.shape[::-1], BF),
            pltpu.SMEM(timestep.shape, jnp.int32),
            pltpu.SMEM(time_weight.shape, F32),
            pltpu.VMEM((128, 128), F32),
            pltpu.VMEM((8, 16, 128), BF),
            pltpu.VMEM((8 * len(FAR), 16, 128), BF),
            pltpu.VMEM((128, 128), F32),
            pltpu.VMEM((4, 32, 128), F32),
            pltpu.VMEM((16, 16, 256), BF),
            pltpu.VMEM((16, NZ, 32, 256), BF),
            dma((8,)),
            dma,
            dma((len(FAR), NX, NC)),
            dma,
            dma((NZ, 2)),
            dma,
            dma((NZ, 2, 4)),
            dma,
            dma,
        ],
        compiler_params=pltpu.CompilerParams(
            collective_id=0, has_side_effects=True, vmem_limit_bytes=62 << 20
        ),
        name="gather_gram",
    )(train_acts, train_grads, timestep, time_weight, query_acts, query_grads, proj_in.T, proj_out.T)
    return pl.pallas_call(
        solve_kernel,
        out_shape=jax.ShapeDtypeStruct((1, 512), F32),
        in_specs=[vmem, vmem, smem],
        out_specs=vmem,
        scratch_shapes=[pltpu.VMEM((512, 128), F32)],
        compiler_params=pltpu.CompilerParams(vmem_limit_bytes=16 << 20),
        name="solve",
    )(gram, cross, damping)


def solution(mesh):
    return jax.shard_map(
        body,
        mesh=mesh,
        in_specs=(
            P("dp", None, None),
            P("dp", None, None),
            P("dp"),
            P(),
            P(("dp", "query"), None, None),
            P(("dp", "query"), None, None),
            P(),
            P(),
            P(),
        ),
        out_specs=P(("dp", "query"), None),
        check_vma=False,
    )
```

```python
import functools

import jax
import jax.numpy as jnp
from jax import lax
from jax.experimental import pallas as pl
from jax.experimental.pallas import tpu as pltpu
from jax.sharding import PartitionSpec as P

MESH = pl.DeviceIdType.MESH
BF = jnp.bfloat16
F32 = jnp.float32

NX, NZ, NC, NY = 4, 16, 2, 4
FAR = (0, 5, -5)
NEAR = {1: (1, 0), -1: (-1, 0), 2: (2, 0), -2: (-2, 0), 6: (1, 5), 4: (-1, 5), -6: (-1, -5),
        -4: (1, -5), 7: (2, 5), 3: (-2, 5), -7: (-2, -5), -3: (2, -5)}
LAST = ((3, 5), (-3, -5))
ORDER = (*FAR, *NEAR, 8)
HALF = len(ORDER) // 2
SCHEDULE = (0, 5, -5, 1, -1, 2, -2, 6, 4, -6, -4, 7, 3, -7, -3, 8)
TOL = 1e-4
MAX_STEPS = 4096


def dot(a, b, dims):
    return lax.dot_general(a, b, (dims, ((), ())), preferred_element_type=F32)


def pair_tiles(m):
    return jnp.concatenate([m[:32], m[32:]], axis=1)


def gram_kernel(
    tacts_hbm, tgrads_hbm, step_hbm, weight_hbm, qacts_hbm, qgrads_hbm, pin_hbm, pout_hbm,
    gram_ref, cross_ref,
    tacts, tgrads, qacts, qgrads, pin, pout, step_ref, weight_ref,
    wide, sendbuf, landing, wide2, spread, query_rows, table, lower_ref,
    load_sem, a_send, a_recv, b_send, b_recv, c_send, c_recv, s_send, s_recv,
):
    dp = lax.axis_index("dp")
    y = lax.axis_index("query")
    x = dp // (NZ * NC)
    z = lax.rem(dp // NC, NZ)
    c = lax.rem(dp, NC)

    def device(dx=0, dz=0, dc=0, dy=0):
        x1 = lax.rem(x + (dx + NX), NX)
        z1 = lax.rem(z + (dz + NZ), NZ)
        c1 = lax.rem(c + dc, NC)
        y1 = lax.rem(y + (dy + NY), NY)
        return ((x1 * NZ + z1) * NC + c1, y1)

    loads = []
    for i, (src, dst) in enumerate(
        [(step_hbm, step_ref), (weight_hbm, weight_ref), (pout_hbm, pout), (tgrads_hbm, tgrads),
         (pin_hbm, pin), (tacts_hbm, tacts), (qgrads_hbm, qgrads), (qacts_hbm, qacts)]
    ):
        copy = pltpu.make_async_copy(src, dst, load_sem.at[i])
        copy.start()
        loads.append(copy)

    barrier = pltpu.get_barrier_semaphore()
    line = [
        (i, dx, dc)
        for i in range(len(FAR)) for dx in range(NX) for dc in range(NC)
        if (i, dx, dc) != (0, 0, 0)
    ]
    partners = [device(dz=FAR[i], dx=dx, dc=dc) for i, dx, dc in line]
    partners += [device(dz=d) for d in (1, -1, 2, -2, 3, -3)]
    partners += [device(dy=d) for d in (1, 2, 3)]
    for partner in partners:
        pl.semaphore_signal(barrier, inc=1, device_id=partner, device_id_type=MESH)

    for i in range(6):
        loads[i].wait()
    count, tok, width_in = tacts.shape
    width_out = tgrads.shape[2]
    grad_proj = dot(tgrads[...].reshape(count * tok, width_out), pout[...], ((1,), (1,))).astype(BF)
    act_proj = dot(tacts[...].reshape(count * tok, width_in), pin[...], ((1,), (1,))).astype(BF)
    for e in range(count):
        rows = slice(e * tok, (e + 1) * tok)
        outer = dot(grad_proj[rows], act_proj[rows], ((0,), (0,)))
        weight = weight_ref[step_ref[e]]
        wide[pl.ds(e, 32, stride=4), :] = pair_tiles(outer * weight)

    def tile_for(x1, c1):
        left = wide[pl.ds(pl.multiple_of(8 * (2 * x1 + c1), 8), 8), :]
        right = wide[pl.ds(pl.multiple_of(64 + 8 * (2 * y + c1), 8), 8), :]
        return jnp.concatenate([left, right], axis=0).astype(BF)

    for x1 in range(NX):
        for c1 in range(NC):
            sendbuf[2 * x1 + c1] = tile_for(x1, c1)
    me = 2 * x + c
    landing[me] = tile_for(x, c)

    pl.semaphore_wait(barrier, len(partners))

    for i, dx, dc in line:
        x1 = lax.rem(x + dx, NX)
        c1 = lax.rem(c + dc, NC)
        pltpu.make_async_remote_copy(
            src_ref=sendbuf.at[2 * x1 + c1], dst_ref=landing.at[8 * i + me],
            send_sem=a_send, recv_sem=a_recv.at[i, dx, dc],
            device_id=device(dz=-FAR[i], dx=dx, dc=dc), device_id_type=MESH,
        ).start()

    loads[6].wait()
    loads[7].wait()
    qg = dot(qgrads[0], pout[...], ((1,), (1,))).astype(BF)
    qa = dot(qacts[0], pin[...], ((1,), (1,))).astype(BF)
    query = pair_tiles(dot(qg, qa, ((0,), (0,))))
    for k in range(16):
        row = jnp.concatenate([query[2 * k:2 * k + 1], query[2 * k + 1:2 * k + 2]], axis=1)
        query_rows[k] = jnp.broadcast_to(row, (16, 256)).astype(BF)

    kx = 2 * x + c
    ky = 8 + 2 * y + c
    sib = device(dc=1)

    def take(i):
        for i1, dx, dc in line:
            if i1 == i:
                src = 2 * lax.rem(x + (NX - dx), NX) + lax.rem(c + dc, NC)
                pltpu.make_async_remote_copy(
                    src_ref=sendbuf.at[0], dst_ref=landing.at[8 * i + src],
                    send_sem=a_send, recv_sem=a_recv.at[i, dx, dc],
                    device_id=sib, device_id_type=MESH,
                ).wait_recv()
        wide2[...] = landing[8 * i:8 * i + 8].astype(F32).reshape(128, 128)
        for t in range(4):
            for e in range(4):
                spread[t, pl.ds(e, 8, stride=4), :] = wide2[pl.ds(4 * t + e, 8, stride=16), :]
        o = ORDER.index(FAR[i])
        table[kx, o] = jnp.concatenate([spread[0], spread[1]], axis=1).astype(BF)
        table[ky, o] = jnp.concatenate([spread[2], spread[3]], axis=1).astype(BF)

    def move(k, o, send_sem, recv_sem, target, to=None):
        slot = ORDER.index(o)
        return pltpu.make_async_remote_copy(
            src_ref=table.at[k, slot],
            dst_ref=table.at[k, slot if to is None else ORDER.index(to)],
            send_sem=send_sem, recv_sem=recv_sem, device_id=target, device_id_type=MESH,
        )

    def relay(s):
        for o, (n, s1) in NEAR.items():
            if s1 == s:
                move(kx, s, b_send, b_recv.at[o + 7, 0], device(dz=-n), o).start()
                move(ky, s, b_send, b_recv.at[o + 7, 1], device(dz=-n), o).start()
        for kind, k in ((0, kx), (1, ky)):
            if LAST[kind][1] == s:
                move(k, s, b_send, b_recv.at[15, kind], device(dz=-LAST[kind][0]), 8).start()

    def relayed(o):
        move(kx, o, b_send, b_recv.at[o + 7, 0], sib).wait_recv()
        move(ky, o, b_send, b_recv.at[o + 7, 1], sib).wait_recv()

    def to_sib(k, o):
        half = ORDER.index(o) // HALF
        move(k, o, s_send, s_recv.at[half], sib).start()

    def fan_out(o):
        for d in (1, 3, 2):
            move(kx, o, c_send, c_recv.at[o + 7, 0, d], device(dx=d)).start()
            move(ky, o, c_send, c_recv.at[o + 7, 1, d], device(dy=d)).start()
        to_sib(kx, o)
        to_sib(ky, o)

    def pass_on(o):
        for d in (1, 3, 2):
            k = 2 * lax.rem(x + (NX - d), NX) + c
            move(k, o, c_send, c_recv.at[o + 7, 0, d], sib).wait_recv()
            to_sib(k, o)
            k = 8 + 2 * lax.rem(y + (NY - d), NY) + c
            move(k, o, c_send, c_recv.at[o + 7, 1, d], sib).wait_recv()
            to_sib(k, o)

    for step in SCHEDULE:
        if step in FAR:
            take(FAR.index(step))
            relay(step)
        else:
            relayed(step)
        fan_out(step)

    def drain(part, sem):
        pltpu.make_async_copy(part, part, sem).wait()

    for o in ORDER[:HALF]:
        pass_on(o)
    drain(table.at[0:4], s_recv.at[0])

    def rows(k, lower):
        part = table[k, HALF:] if lower else table[k, :HALF]
        return part.reshape(256, 256)

    def first(i, total):
        upper = jnp.concatenate([rows(4 * i + k, False) for k in range(4)], axis=1)
        return total + dot(upper, upper, ((1,), (1,)))

    gram_ref[:256, :256] = lax.fori_loop(0, 4, first, jnp.zeros((256, 256), F32))

    for o in ORDER[HALF:]:
        pass_on(o)
    drain(table.at[0:4], s_recv.at[1])

    lower_ref[...] = jnp.zeros_like(lower_ref)

    def second(i, carry):
        upper = jnp.concatenate([rows(4 * i + k, False) for k in range(4)], axis=1)
        lower = jnp.concatenate([rows(4 * i + k, True) for k in range(4)], axis=1)
        queries = jnp.concatenate([query_rows[4 * i + k] for k in range(4)], axis=1)
        left = jnp.concatenate([lower, queries], axis=0)
        lower_ref[:, :256] += dot(left, upper, ((1,), (1,)))
        lower_ref[:, 256:] += dot(left, lower, ((1,), (1,)))
        return carry

    lax.fori_loop(0, 4, second, 0)
    gram_ref[256:] = lower_ref[:256]
    gram_ref[:256, 256:] = lower_ref[:256, :256].T
    cross_ref[...] = lower_ref[256:264]

    drain(landing.at[0:len(line)], a_send)
    drain(table.at[0:2, 0:len(NEAR) + 1], b_send)
    drain(table.at[0:6], c_send)
    drain(table.at[0:8], s_send)


def solve_kernel(gram_ref, cross_ref, damping_ref, out_ref, column, ordered):
    rank2 = 4096.0
    eye = (
        lax.broadcasted_iota(jnp.int32, (128, 128), 0)
        == lax.broadcasted_iota(jnp.int32, (128, 128), 1)
    )
    diagonal = jnp.concatenate(
        [
            jnp.sum(
                jnp.where(eye, gram_ref[128 * t:128 * t + 128, 128 * t:128 * t + 128], 0.0),
                axis=0, keepdims=True,
            )
            for t in range(4)
        ],
        axis=1,
    )

    def total(v):
        return jnp.sum(v, axis=1, keepdims=True)

    lam = damping_ref[0] * total(diagonal) / rank2
    top = jnp.max(diagonal, axis=1, keepdims=True) + lam
    scale = 1.0 / top
    lam_scaled = lam * scale
    jacobi = 1.0 / (diagonal * scale + lam_scaled)
    size = jnp.max(jnp.abs(cross_ref[0:1]), axis=1, keepdims=True)
    size = jnp.where(size > 0.0, size, 1.0)
    bound = (TOL * lam_scaled) * (TOL * lam_scaled)

    def product(p):
        parts = [jnp.zeros((8, 128), F32) for _ in range(4)]
        for t in range(4):
            chunk = p[:, 128 * t:128 * t + 128]
            spread = jnp.broadcast_to(chunk, (128, 128)).T
            for u in range(4):
                tile = gram_ref[128 * t:128 * t + 128, 128 * u:128 * u + 128] * spread
                parts[u] += jnp.sum(tile.reshape(16, 8, 128), axis=0)
        whole = jnp.concatenate([jnp.sum(v, axis=0, keepdims=True) for v in parts], axis=1)
        return whole * scale + lam_scaled * p

    def go_on(state):
        step, more = state[0], state[1]
        return jnp.logical_and(step < MAX_STEPS, more)

    def advance(state):
        step, _, s, r, p, v, old_rz, old_alpha = state
        more = (total(r * r) - bound * total(s * s))[0, 0] > 0.0
        u = r * jacobi
        rz = total(r * u)
        beta = rz / old_rz
        w = product(u)
        curve = total(w * u) - beta * rz / old_alpha
        good = curve > 0.0
        alpha = jnp.where(good, rz / curve, 0.0)
        p = u + beta * p
        v = w + beta * v
        old_rz = jnp.where(good, rz, jnp.inf)
        old_alpha = jnp.where(good, alpha, 1.0)
        return step + 1, more, s + alpha * p, r - alpha * v, p, v, old_rz, old_alpha

    r = cross_ref[0:1] / size
    zero = jnp.zeros_like(r)
    one = jnp.ones((1, 1), F32)
    state = (jnp.int32(0), jnp.bool_(True), zero, r, zero, zero, jnp.inf * one, one)
    s = lax.while_loop(go_on, advance, state)[2] * (size * scale)

    z = lax.rem(lax.axis_index("dp") // NC, NZ)
    for t in range(4):
        column[128 * t:128 * t + 128, :] = jnp.broadcast_to(s[:, 128 * t:128 * t + 128], (128, 128)).T
    for slot, o in enumerate(ORDER):
        at = pl.multiple_of(8 * lax.rem(z + (o + NZ), NZ), 8)
        for x in range(NX):
            ordered[pl.ds(128 * x + at, 8), :] = column[32 * slot + 8 * x:32 * slot + 8 * x + 8, :]
    for x in range(NX):
        out_ref[:, 128 * x:128 * x + 128] = ordered[128 * x:128 * x + 128, :].T[0:1, :]


def body(
    train_acts, train_grads, timestep, time_weight, query_acts, query_grads, proj_in, proj_out,
    damping,
):
    hbm = pl.BlockSpec(memory_space=pltpu.HBM)
    smem = pl.BlockSpec(memory_space=pltpu.SMEM)
    vmem = pl.BlockSpec(memory_space=pltpu.VMEM)
    dma = pltpu.SemaphoreType.DMA
    gram, cross = pl.pallas_call(
        gram_kernel,
        out_shape=(
            jax.ShapeDtypeStruct((512, 512), F32),
            jax.ShapeDtypeStruct((8, 512), F32),
        ),
        in_specs=[hbm] * 8,
        out_specs=(vmem, vmem),
        scratch_shapes=[
            pltpu.VMEM(train_acts.shape, BF),
            pltpu.VMEM(train_grads.shape, BF),
            pltpu.VMEM(query_acts.shape, BF),
            pltpu.VMEM(query_grads.shape, BF),
            pltpu.VMEM(proj_in.shape[::-1], BF),
            pltpu.VMEM(proj_out.shape[::-1], BF),
            pltpu.SMEM(timestep.shape, jnp.int32),
            pltpu.SMEM(time_weight.shape, F32),
            pltpu.VMEM((128, 128), F32),
            pltpu.VMEM((8, 16, 128), BF),
            pltpu.VMEM((8 * len(FAR), 16, 128), BF),
            pltpu.VMEM((128, 128), F32),
            pltpu.VMEM((4, 32, 128), F32),
            pltpu.VMEM((16, 16, 256), BF),
            pltpu.VMEM((16, NZ, 32, 256), BF),
            pltpu.VMEM((272, 512), F32),
            dma((8,)),
            dma,
            dma((len(FAR), NX, NC)),
            dma,
            dma((NZ, 2)),
            dma,
            dma((NZ, 2, 4)),
            dma,
            dma((2,)),
        ],
        compiler_params=pltpu.CompilerParams(
            collective_id=0, has_side_effects=True, vmem_limit_bytes=40 << 20
        ),
        name="gather_gram",
    )(
        *[
            pltpu.with_memory_space_constraint(operand, pltpu.HBM)
            for operand in (
                train_acts, train_grads, timestep, time_weight, query_acts, query_grads,
                proj_in.T, proj_out.T,
            )
        ]
    )
    return pl.pallas_call(
        solve_kernel,
        out_shape=jax.ShapeDtypeStruct((1, 512), F32),
        in_specs=[vmem, vmem, smem],
        out_specs=vmem,
        scratch_shapes=[pltpu.VMEM((512, 128), F32)] * 2,
        compiler_params=pltpu.CompilerParams(vmem_limit_bytes=16 << 20),
        name="solve",
    )(gram, cross, damping)


def solution(mesh):
    return jax.shard_map(
        body,
        mesh=mesh,
        in_specs=(
            P("dp", None, None),
            P("dp", None, None),
            P("dp"),
            P(),
            P(("dp", "query"), None, None),
            P(("dp", "query"), None, None),
            P(),
            P(),
            P(),
        ),
        out_specs=P(("dp", "query"), None),
        check_vma=False,
    )
```

```python
import functools

import jax
import jax.numpy as jnp
from jax import lax
from jax.experimental import pallas as pl
from jax.experimental.pallas import tpu as pltpu
from jax.sharding import PartitionSpec as P

MESH = pl.DeviceIdType.MESH
BF = jnp.bfloat16
F32 = jnp.float32

NX, NZ, NC, NY = 4, 16, 2, 4
FAR = (0, 5, -5)
NEAR = {1: (1, 0), -1: (-1, 0), 2: (2, 0), -2: (-2, 0), 6: (1, 5), 4: (-1, 5), -6: (-1, -5), -4: (1, -5), 3: (1, 2), -3: (-1, -2), 7: (1, 6), -7: (-1, -6)}
LAST = ((2, 6), (-2, -6))
ORDER = (*FAR, *NEAR, 8)
HALF = len(ORDER) // 2
SCHEDULE = (0, 1, -1, 5, -5, 2, -2, 6, -6, 4, -4, 3, -3, 7, -7, 8)
TOL = 1e-4
MAX_STEPS = 4096


def dot(a, b, dims):
    return lax.dot_general(a, b, (dims, ((), ())), preferred_element_type=F32)


def pair_tiles(m):
    return jnp.concatenate([m[:32], m[32:]], axis=1)


def gram_kernel(
    tacts_hbm, tgrads_hbm, step_hbm, weight_hbm, qacts_hbm, qgrads_hbm, pin_hbm, pout_hbm,
    gram_ref, cross_ref,
    tacts, tgrads, qacts, qgrads, pin, pout, step_ref, weight_ref,
    wide, sendbuf, landing, wide2, spread, query_rows, sib_query, both, table,
    part0, part1, part2, inbox0, inbox1, inbox2,
    load_sem, a_send, a_recv, b_send, b_recv, c_send, c_recv, q_send, q_recv, s_send, s_recv,
):
    dp = lax.axis_index("dp")
    y = lax.axis_index("query")
    x = dp // (NZ * NC)
    z = lax.rem(dp // NC, NZ)
    c = lax.rem(dp, NC)

    def device(dx=0, dz=0, dc=0, dy=0):
        x1 = lax.rem(x + (dx + NX), NX)
        z1 = lax.rem(z + (dz + NZ), NZ)
        c1 = lax.rem(c + dc, NC)
        y1 = lax.rem(y + (dy + NY), NY)
        return ((x1 * NZ + z1) * NC + c1, y1)

    loads = []
    for i, (src, dst) in enumerate(
        [(step_hbm, step_ref), (weight_hbm, weight_ref), (pout_hbm, pout), (tgrads_hbm, tgrads),
         (pin_hbm, pin), (tacts_hbm, tacts), (qgrads_hbm, qgrads), (qacts_hbm, qacts)]
    ):
        copy = pltpu.make_async_copy(src, dst, load_sem.at[i])
        copy.start()
        loads.append(copy)

    barrier = pltpu.get_barrier_semaphore()
    line = [
        (i, dx, dc)
        for i in range(len(FAR)) for dx in range(NX) for dc in range(NC)
        if (i, dx, dc) != (0, 0, 0)
    ]
    partners = [device(dz=FAR[i], dx=dx, dc=dc) for i, dx, dc in line]
    partners += [device(dz=d) for d in (1, -1, 2, -2, 3, -3)]
    partners += [device(dy=d) for d in (1, 2, 3)]
    for partner in partners:
        pl.semaphore_signal(barrier, inc=1, device_id=partner, device_id_type=MESH)

    count, tok, width_in = tacts.shape
    width_out = tgrads.shape[2]
    loads[2].wait()
    loads[3].wait()
    grad_proj = dot(tgrads[...].reshape(count * tok, width_out), pout[...], ((1,), (1,))).astype(BF)
    loads[4].wait()
    loads[5].wait()
    act_proj = dot(tacts[...].reshape(count * tok, width_in), pin[...], ((1,), (1,))).astype(BF)
    loads[0].wait()
    loads[1].wait()
    for e in range(count):
        rows = slice(e * tok, (e + 1) * tok)
        outer = dot(grad_proj[rows], act_proj[rows], ((0,), (0,)))
        weight = weight_ref[step_ref[e]]
        wide[pl.ds(e, 32, stride=4), :] = pair_tiles(outer * weight)

    def tile_for(x1, c1):
        left = wide[pl.ds(pl.multiple_of(8 * (2 * x1 + c1), 8), 8), :]
        right = wide[pl.ds(pl.multiple_of(64 + 8 * (2 * y + c1), 8), 8), :]
        return jnp.concatenate([left, right], axis=0).astype(BF)

    for x1 in range(NX):
        for c1 in range(NC):
            sendbuf[2 * x1 + c1] = tile_for(x1, c1)
    me = 2 * x + c
    landing[me] = tile_for(x, c)

    pl.semaphore_wait(barrier, len(partners))

    for i, dx, dc in line:
        x1 = lax.rem(x + dx, NX)
        c1 = lax.rem(c + dc, NC)
        pltpu.make_async_remote_copy(
            src_ref=sendbuf.at[2 * x1 + c1], dst_ref=landing.at[8 * i + me],
            send_sem=a_send, recv_sem=a_recv.at[i],
            device_id=device(dz=-FAR[i], dx=dx, dc=dc), device_id_type=MESH,
        ).start()

    loads[6].wait()
    loads[7].wait()
    qg = dot(qgrads[0], pout[...], ((1,), (1,))).astype(BF)
    qa = dot(qacts[0], pin[...], ((1,), (1,))).astype(BF)
    query = pair_tiles(dot(qg, qa, ((0,), (0,))))
    for k in range(16):
        row = jnp.concatenate([query[2 * k:2 * k + 1], query[2 * k + 1:2 * k + 2]], axis=1)
        query_rows[k % 2, k // 2] = jnp.broadcast_to(row, (16, 256)).astype(BF)
    sib = device(dc=1)
    query_copy = pltpu.make_async_remote_copy(
        src_ref=query_rows.at[1 - c], dst_ref=sib_query, send_sem=q_send, recv_sem=q_recv,
        device_id=sib, device_id_type=MESH,
    )
    query_copy.start()

    kx = x
    ky = NX + y

    def drain(part, sem):
        pltpu.make_async_copy(part, part, sem).wait()

    def take(i):
        drain(landing.at[0:sum(i1 == i for i1, _, _ in line)], a_recv.at[i])
        wide2[...] = landing[8 * i:8 * i + 8].astype(F32).reshape(128, 128)
        for t in range(4):
            for e in range(4):
                spread[t, pl.ds(e, 8, stride=4), :] = wide2[pl.ds(4 * t + e, 8, stride=16), :]
        o = ORDER.index(FAR[i])
        table[kx, o] = jnp.concatenate([spread[0], spread[1]], axis=1).astype(BF)
        table[ky, o] = jnp.concatenate([spread[2], spread[3]], axis=1).astype(BF)

    def move(k, o, send_sem, recv_sem, target, to=None):
        slot = ORDER.index(o)
        return pltpu.make_async_remote_copy(
            src_ref=table.at[k, slot],
            dst_ref=table.at[k, slot if to is None else ORDER.index(to)],
            send_sem=send_sem, recv_sem=recv_sem, device_id=target, device_id_type=MESH,
        )

    def relay(s):
        for o, (n, s1) in NEAR.items():
            if s1 == s:
                move(kx, s, b_send, b_recv.at[ORDER.index(o)], device(dz=-n), o).start()
                move(ky, s, b_send, b_recv.at[ORDER.index(o)], device(dz=-n), o).start()
        for kind, k in ((0, kx), (1, ky)):
            if LAST[kind][1] == s:
                move(k, s, b_send, b_recv.at[ORDER.index(8)], device(dz=-LAST[kind][0]), 8).start()

    def relayed(o):
        drain(table.at[0, 0:2], b_recv.at[ORDER.index(o)])

    def fan_out(o):
        for d in (1, 3, 2):
            move(kx, o, c_send, c_recv.at[ORDER.index(o)], device(dx=d)).start()
            move(ky, o, c_send, c_recv.at[ORDER.index(o)], device(dy=d)).start()

    def spread_out(o):
        drain(table.at[0, 0:6], c_recv.at[ORDER.index(o)])

    for step in SCHEDULE:
        if step in FAR:
            take(FAR.index(step))
        else:
            relayed(step)
        relay(step)
        fan_out(step)

    def exchange(i, mine, theirs):
        copy = pltpu.make_async_remote_copy(
            src_ref=mine, dst_ref=theirs, send_sem=s_send.at[i], recv_sem=s_recv.at[i],
            device_id=sib, device_id_type=MESH,
        )
        copy.start()
        return copy

    def rows(i, lower):
        parts = [table[4 * i + k, HALF:] if lower else table[4 * i + k, :HALF] for k in range(4)]
        return jnp.concatenate([part.reshape(256, 256) for part in parts], axis=1)

    for o in ORDER[:HALF]:
        spread_out(o)
    query_copy.wait()
    own_row = lax.broadcasted_iota(jnp.int32, (16, 256), 0) < 8
    for k in range(8):
        both[k] = jnp.where(
            own_row, query_rows[c, k].astype(F32), sib_query[k].astype(F32)
        ).astype(BF)

    def queries(i):
        return jnp.concatenate([both[4 * i + k] for k in range(4)], axis=1)

    upper = [rows(i, False) for i in range(2)]
    part0[...] = dot(upper[0], upper[0], ((1,), (1,))) + dot(upper[1], upper[1], ((1,), (1,)))
    copies = [exchange(0, part0, inbox0)]

    for o in ORDER[HALF:]:
        spread_out(o)
    left = [jnp.concatenate([rows(i, True), queries(i)], axis=0) for i in range(2)]
    upper = [rows(i, False) for i in range(2)]
    part1[...] = dot(left[0], upper[0], ((1,), (1,))) + dot(left[1], upper[1], ((1,), (1,)))
    copies.append(exchange(1, part1, inbox1))
    left = [jnp.concatenate([rows(i, True), queries(i)], axis=0) for i in range(2)]
    part2[...] = dot(left[0], left[0][:256], ((1,), (1,))) + dot(left[1], left[1][:256], ((1,), (1,)))
    copies.append(exchange(2, part2, inbox2))

    copies[0].wait_recv()
    gram_ref[:256, :256] = part0[...] + inbox0[...]
    copies[1].wait_recv()
    corner = part1[:256] + inbox1[:256]
    gram_ref[256:, :256] = corner
    gram_ref[:256, 256:] = corner.T
    cross_ref[:, :256] = part1[256:264] + inbox1[264:272]
    copies[2].wait_recv()
    gram_ref[256:, 256:] = part2[:256] + inbox2[:256]
    cross_ref[:, 256:] = part2[256:264] + inbox2[264:272]

    drain(landing.at[0:len(line)], a_send)
    drain(table.at[0:2, 0:len(NEAR) + 1], b_send)
    drain(table.at[0:6], c_send)
    for copy in copies:
        copy.wait_send()


def solve_kernel(gram_ref, cross_ref, damping_ref, out_ref, column, ordered):
    rank2 = 4096.0
    eye = (
        lax.broadcasted_iota(jnp.int32, (128, 128), 0)
        == lax.broadcasted_iota(jnp.int32, (128, 128), 1)
    )
    diagonal = jnp.concatenate(
        [
            jnp.sum(
                jnp.where(eye, gram_ref[128 * t:128 * t + 128, 128 * t:128 * t + 128], 0.0),
                axis=0, keepdims=True,
            )
            for t in range(4)
        ],
        axis=1,
    )

    def total(v):
        return jnp.sum(v, axis=1, keepdims=True)

    lam = damping_ref[0] * total(diagonal) / rank2
    top = jnp.max(diagonal, axis=1, keepdims=True) + lam
    scale = 1.0 / top
    lam_scaled = lam * scale
    jacobi = 1.0 / (diagonal * scale + lam_scaled)
    size = jnp.max(jnp.abs(cross_ref[0:1]), axis=1, keepdims=True)
    size = jnp.where(size > 0.0, size, 1.0)
    bound = (TOL * lam_scaled) * (TOL * lam_scaled)

    def product(p):
        parts = [jnp.zeros((8, 128), F32) for _ in range(4)]
        for t in range(4):
            chunk = p[:, 128 * t:128 * t + 128]
            spread = jnp.broadcast_to(chunk, (128, 128)).T
            for u in range(4):
                tile = gram_ref[128 * t:128 * t + 128, 128 * u:128 * u + 128] * spread
                parts[u] += jnp.sum(tile.reshape(16, 8, 128), axis=0)
        whole = jnp.concatenate([jnp.sum(v, axis=0, keepdims=True) for v in parts], axis=1)
        return whole * scale + lam_scaled * p

    def go_on(state):
        step, more = state[0], state[1]
        return jnp.logical_and(step < MAX_STEPS, more)

    def advance(state):
        step, _, s, r, p, v, old_rz, old_alpha = state
        more = (total(r * r) - bound * total(s * s))[0, 0] > 0.0
        u = r * jacobi
        rz = total(r * u)
        beta = rz / old_rz
        w = product(u)
        curve = total(w * u) - beta * rz / old_alpha
        good = curve > 0.0
        alpha = jnp.where(good, rz / curve, 0.0)
        p = u + beta * p
        v = w + beta * v
        old_rz = jnp.where(good, rz, jnp.inf)
        old_alpha = jnp.where(good, alpha, 1.0)
        return step + 1, more, s + alpha * p, r - alpha * v, p, v, old_rz, old_alpha

    r = cross_ref[0:1] / size
    zero = jnp.zeros_like(r)
    one = jnp.ones((1, 1), F32)
    state = (jnp.int32(0), jnp.bool_(True), zero, r, zero, zero, jnp.inf * one, one)
    s = lax.while_loop(go_on, advance, state)[2] * (size * scale)

    z = lax.rem(lax.axis_index("dp") // NC, NZ)
    for t in range(4):
        column[128 * t:128 * t + 128, :] = jnp.broadcast_to(s[:, 128 * t:128 * t + 128], (128, 128)).T
    for slot, o in enumerate(ORDER):
        at = pl.multiple_of(8 * lax.rem(z + (o + NZ), NZ), 8)
        for x in range(NX):
            ordered[pl.ds(128 * x + at, 8), :] = column[32 * slot + 8 * x:32 * slot + 8 * x + 8, :]
    for x in range(NX):
        out_ref[:, 128 * x:128 * x + 128] = ordered[128 * x:128 * x + 128, :].T[0:1, :]


def body(
    train_acts, train_grads, timestep, time_weight, query_acts, query_grads, proj_in, proj_out,
    damping,
):
    hbm = pl.BlockSpec(memory_space=pltpu.HBM)
    smem = pl.BlockSpec(memory_space=pltpu.SMEM)
    vmem = pl.BlockSpec(memory_space=pltpu.VMEM)
    dma = pltpu.SemaphoreType.DMA
    gram, cross = pl.pallas_call(
        gram_kernel,
        out_shape=(
            jax.ShapeDtypeStruct((512, 512), F32),
            jax.ShapeDtypeStruct((8, 512), F32),
        ),
        in_specs=[hbm] * 8,
        out_specs=(vmem, vmem),
        scratch_shapes=[
            pltpu.VMEM(train_acts.shape, BF),
            pltpu.VMEM(train_grads.shape, BF),
            pltpu.VMEM(query_acts.shape, BF),
            pltpu.VMEM(query_grads.shape, BF),
            pltpu.VMEM(proj_in.shape[::-1], BF),
            pltpu.VMEM(proj_out.shape[::-1], BF),
            pltpu.SMEM(timestep.shape, jnp.int32),
            pltpu.SMEM(time_weight.shape, F32),
            pltpu.VMEM((128, 128), F32),
            pltpu.VMEM((8, 16, 128), BF),
            pltpu.VMEM((8 * len(FAR), 16, 128), BF),
            pltpu.VMEM((128, 128), F32),
            pltpu.VMEM((4, 32, 128), F32),
            pltpu.VMEM((2, 8, 16, 256), BF),
            pltpu.VMEM((8, 16, 256), BF),
            pltpu.VMEM((8, 16, 256), BF),
            pltpu.VMEM((8, NZ, 32, 256), BF),
            pltpu.VMEM((256, 256), F32),
            pltpu.VMEM((272, 256), F32),
            pltpu.VMEM((272, 256), F32),
            pltpu.VMEM((256, 256), F32),
            pltpu.VMEM((272, 256), F32),
            pltpu.VMEM((272, 256), F32),
            dma((8,)),
            dma,
            dma((len(FAR),)),
            dma,
            dma((NZ,)),
            dma,
            dma((NZ,)),
            dma,
            dma,
            dma((3,)),
            dma((3,)),
        ],
        compiler_params=pltpu.CompilerParams(
            collective_id=0, has_side_effects=True, vmem_limit_bytes=40 << 20
        ),
        name="gather_gram",
    )(
        *[
            pltpu.with_memory_space_constraint(operand, pltpu.HBM)
            for operand in (
                train_acts, train_grads, timestep, time_weight, query_acts, query_grads,
                proj_in.T, proj_out.T,
            )
        ]
    )
    return pl.pallas_call(
        solve_kernel,
        out_shape=jax.ShapeDtypeStruct((1, 512), F32),
        in_specs=[vmem, vmem, smem],
        out_specs=vmem,
        scratch_shapes=[pltpu.VMEM((512, 128), F32)] * 2,
        compiler_params=pltpu.CompilerParams(vmem_limit_bytes=16 << 20),
        name="solve",
    )(gram, cross, damping)


def solution(mesh):
    return jax.shard_map(
        body,
        mesh=mesh,
        in_specs=(
            P("dp", None, None),
            P("dp", None, None),
            P("dp"),
            P(),
            P(("dp", "query"), None, None),
            P(("dp", "query"), None, None),
            P(),
            P(),
            P(),
        ),
        out_specs=P(("dp", "query"), None),
        check_vma=False,
    )
```

```python
import functools

import jax
import jax.numpy as jnp
from jax import lax
from jax.experimental import pallas as pl
from jax.experimental.pallas import tpu as pltpu
from jax.sharding import PartitionSpec as P

MESH = pl.DeviceIdType.MESH
BF = jnp.bfloat16
F32 = jnp.float32

NX, NZ, NC, NY = 4, 16, 2, 4
FAR = (0, 5, -5)
NEAR = {1: (1, 0), -1: (-1, 0), 2: (2, 0), -2: (-2, 0), 6: (1, 5), 4: (-1, 5), -6: (-1, -5), -4: (1, -5), 3: (1, 2), -3: (-1, -2), 7: (1, 6), -7: (-1, -6)}
LAST = ((2, 6), (-2, -6))
ORDER = (*FAR, *NEAR, 8)
HALF = len(ORDER) // 2
SCHEDULE = (0, 1, -1, 5, -5, 2, -2, 6, -6, 4, -4, 3, -3, 7, -7, 8)
TOL = 1e-4
MAX_STEPS = 4096


def dot(a, b, dims):
    return lax.dot_general(a, b, (dims, ((), ())), preferred_element_type=F32)


def pair_tiles(m):
    return jnp.concatenate([m[:32], m[32:]], axis=1)


def gram_kernel(
    tacts_hbm, tgrads_hbm, step_hbm, weight_hbm, qacts_hbm, qgrads_hbm, pin_hbm, pout_hbm,
    gram_ref, cross_ref,
    tacts, tgrads, qacts, qgrads, pin, pout, step_ref, weight_ref,
    wide, sendbuf, landing, wide2, spread, query_rows, sib_query, both, table,
    part0, part1, part2, inbox0, inbox1, inbox2,
    load_sem, a_send, a_recv, b_send, b_recv, c_send, c_recv, q_send, q_recv, s_send, s_recv,
):
    dp = lax.axis_index("dp")
    y = lax.axis_index("query")
    x = dp // (NZ * NC)
    z = lax.rem(dp // NC, NZ)
    c = lax.rem(dp, NC)

    def device(dx=0, dz=0, dc=0, dy=0):
        x1 = lax.rem(x + (dx + NX), NX)
        z1 = lax.rem(z + (dz + NZ), NZ)
        c1 = lax.rem(c + dc, NC)
        y1 = lax.rem(y + (dy + NY), NY)
        return ((x1 * NZ + z1) * NC + c1, y1)

    loads = []
    for i, (src, dst) in enumerate(
        [(step_hbm, step_ref), (weight_hbm, weight_ref), (pout_hbm, pout), (tgrads_hbm, tgrads),
         (pin_hbm, pin), (tacts_hbm, tacts), (qgrads_hbm, qgrads), (qacts_hbm, qacts)]
    ):
        copy = pltpu.make_async_copy(src, dst, load_sem.at[i])
        copy.start()
        loads.append(copy)

    barrier = pltpu.get_barrier_semaphore()
    line = [
        (i, dx, dc)
        for i in range(len(FAR)) for dx in range(NX) for dc in range(NC)
        if (i, dx, dc) != (0, 0, 0)
    ]
    partners = [device(dz=FAR[i], dx=dx, dc=dc) for i, dx, dc in line]
    partners += [device(dz=d) for d in (1, -1, 2, -2)]
    partners += [device(dy=d) for d in (1, 2, 3)]
    for partner in partners:
        pl.semaphore_signal(barrier, inc=1, device_id=partner, device_id_type=MESH)

    count, tok, width_in = tacts.shape
    width_out = tgrads.shape[2]
    loads[2].wait()
    loads[3].wait()
    grad_proj = dot(tgrads[...].reshape(count * tok, width_out), pout[...], ((1,), (1,))).astype(BF)
    loads[4].wait()
    loads[5].wait()
    act_proj = dot(tacts[...].reshape(count * tok, width_in), pin[...], ((1,), (1,))).astype(BF)
    loads[0].wait()
    loads[1].wait()
    for e in range(count):
        rows = slice(e * tok, (e + 1) * tok)
        outer = dot(grad_proj[rows], act_proj[rows], ((0,), (0,)))
        weight = weight_ref[step_ref[e]]
        wide[pl.ds(e, 32, stride=4), :] = pair_tiles(outer * weight)

    def tile_for(x1, c1):
        left = wide[pl.ds(pl.multiple_of(8 * (2 * x1 + c1), 8), 8), :]
        right = wide[pl.ds(pl.multiple_of(64 + 8 * (2 * y + c1), 8), 8), :]
        return jnp.concatenate([left, right], axis=0).astype(BF)

    for x1 in range(NX):
        for c1 in range(NC):
            sendbuf[2 * x1 + c1] = tile_for(x1, c1)
    me = 2 * x + c
    landing[me] = tile_for(x, c)

    pl.semaphore_wait(barrier, len(partners))

    for i, dx, dc in line:
        x1 = lax.rem(x + dx, NX)
        c1 = lax.rem(c + dc, NC)
        pltpu.make_async_remote_copy(
            src_ref=sendbuf.at[2 * x1 + c1], dst_ref=landing.at[8 * i + me],
            send_sem=a_send, recv_sem=a_recv.at[i],
            device_id=device(dz=-FAR[i], dx=dx, dc=dc), device_id_type=MESH,
        ).start()

    loads[6].wait()
    loads[7].wait()
    qg = dot(qgrads[0], pout[...], ((1,), (1,))).astype(BF)
    qa = dot(qacts[0], pin[...], ((1,), (1,))).astype(BF)
    query = pair_tiles(dot(qg, qa, ((0,), (0,))))
    for k in range(16):
        row = jnp.concatenate([query[2 * k:2 * k + 1], query[2 * k + 1:2 * k + 2]], axis=1)
        query_rows[k % 2, k // 2] = jnp.broadcast_to(row, (16, 256)).astype(BF)
    sib = device(dc=1)
    query_copy = pltpu.make_async_remote_copy(
        src_ref=query_rows.at[1 - c], dst_ref=sib_query, send_sem=q_send, recv_sem=q_recv,
        device_id=sib, device_id_type=MESH,
    )
    query_copy.start()

    kx = x
    ky = NX + y

    def drain(part, sem):
        pltpu.make_async_copy(part, part, sem).wait()

    def take(i):
        drain(landing.at[0:sum(i1 == i for i1, _, _ in line)], a_recv.at[i])
        wide2[...] = landing[8 * i:8 * i + 8].astype(F32).reshape(128, 128)
        for t in range(4):
            for e in range(4):
                spread[t, pl.ds(e, 8, stride=4), :] = wide2[pl.ds(4 * t + e, 8, stride=16), :]
        o = ORDER.index(FAR[i])
        table[kx, o] = jnp.concatenate([spread[0], spread[1]], axis=1).astype(BF)
        table[ky, o] = jnp.concatenate([spread[2], spread[3]], axis=1).astype(BF)

    def move(k, o, send_sem, recv_sem, target, to=None):
        slot = ORDER.index(o)
        return pltpu.make_async_remote_copy(
            src_ref=table.at[k, slot],
            dst_ref=table.at[k, slot if to is None else ORDER.index(to)],
            send_sem=send_sem, recv_sem=recv_sem, device_id=target, device_id_type=MESH,
        )

    def relay(s):
        for o, (n, s1) in NEAR.items():
            if s1 == s:
                move(kx, s, b_send, b_recv.at[ORDER.index(o) - len(FAR)], device(dz=-n), o).start()
                move(ky, s, b_send, b_recv.at[ORDER.index(o) - len(FAR)], device(dz=-n), o).start()
        for kind, k in ((0, kx), (1, ky)):
            if LAST[kind][1] == s:
                move(k, s, b_send, b_recv.at[ORDER.index(8) - len(FAR)], device(dz=-LAST[kind][0]), 8).start()

    def relayed(o):
        drain(table.at[0, 0:2], b_recv.at[ORDER.index(o) - len(FAR)])

    def fan_out(o):
        for d in (1, 3, 2):
            move(kx, o, c_send, c_recv.at[ORDER.index(o) // HALF], device(dx=d)).start()
            move(ky, o, c_send, c_recv.at[ORDER.index(o) // HALF], device(dy=d)).start()

    for step in SCHEDULE:
        if step in FAR:
            take(FAR.index(step))
        else:
            relayed(step)
        relay(step)
        fan_out(step)

    def exchange(i, mine, theirs):
        copy = pltpu.make_async_remote_copy(
            src_ref=mine, dst_ref=theirs, send_sem=s_send.at[i], recv_sem=s_recv.at[i],
            device_id=sib, device_id_type=MESH,
        )
        copy.start()
        return copy

    def rows(i, lower):
        parts = [table[4 * i + k, HALF:] if lower else table[4 * i + k, :HALF] for k in range(4)]
        return jnp.concatenate([part.reshape(256, 256) for part in parts], axis=1)

    drain(table.at[0:3], c_recv.at[0])
    query_copy.wait()
    own_row = lax.broadcasted_iota(jnp.int32, (16, 256), 0) < 8
    for k in range(8):
        both[k] = jnp.where(
            own_row, query_rows[c, k].astype(F32), sib_query[k].astype(F32)
        ).astype(BF)

    def queries(i):
        return jnp.concatenate([both[4 * i + k] for k in range(4)], axis=1)

    upper = [rows(i, False) for i in range(2)]
    part0[...] = dot(upper[0], upper[0], ((1,), (1,))) + dot(upper[1], upper[1], ((1,), (1,)))
    copies = [exchange(0, part0, inbox0)]

    drain(table.at[0:3], c_recv.at[1])
    left = [jnp.concatenate([rows(i, True), queries(i)], axis=0) for i in range(2)]
    upper = [rows(i, False) for i in range(2)]
    part1[...] = dot(left[0], upper[0], ((1,), (1,))) + dot(left[1], upper[1], ((1,), (1,)))
    copies.append(exchange(1, part1, inbox1))
    left = [jnp.concatenate([rows(i, True), queries(i)], axis=0) for i in range(2)]
    part2[...] = dot(left[0], left[0][:256], ((1,), (1,))) + dot(left[1], left[1][:256], ((1,), (1,)))
    copies.append(exchange(2, part2, inbox2))

    copies[0].wait_recv()
    gram_ref[:256, :256] = part0[...] + inbox0[...]
    copies[1].wait_recv()
    corner = part1[:256] + inbox1[:256]
    gram_ref[256:, :256] = corner
    gram_ref[:256, 256:] = corner.T
    cross_ref[:, :256] = part1[256:264] + inbox1[264:272]
    copies[2].wait_recv()
    gram_ref[256:, 256:] = part2[:256] + inbox2[:256]
    cross_ref[:, 256:] = part2[256:264] + inbox2[264:272]

    drain(landing.at[0:len(line)], a_send)
    drain(table.at[0:2, 0:len(NEAR) + 1], b_send)
    drain(table.at[0:6], c_send)
    for copy in copies:
        copy.wait_send()


def solve_kernel(gram_ref, cross_ref, damping_ref, out_ref, column, ordered):
    rank2 = 4096.0
    eye = (
        lax.broadcasted_iota(jnp.int32, (128, 128), 0)
        == lax.broadcasted_iota(jnp.int32, (128, 128), 1)
    )
    diagonal = jnp.concatenate(
        [
            jnp.sum(
                jnp.where(eye, gram_ref[128 * t:128 * t + 128, 128 * t:128 * t + 128], 0.0),
                axis=0, keepdims=True,
            )
            for t in range(4)
        ],
        axis=1,
    )

    def total(v):
        return jnp.sum(v, axis=1, keepdims=True)

    lam = damping_ref[0] * total(diagonal) / rank2
    top = jnp.max(diagonal, axis=1, keepdims=True) + lam
    scale = 1.0 / top
    lam_scaled = lam * scale
    jacobi = 1.0 / (diagonal * scale + lam_scaled)
    size = jnp.max(jnp.abs(cross_ref[0:1]), axis=1, keepdims=True)
    size = jnp.where(size > 0.0, size, 1.0)
    bound = (TOL * lam_scaled) * (TOL * lam_scaled)

    def product(p):
        parts = [jnp.zeros((8, 128), F32) for _ in range(4)]
        for t in range(4):
            chunk = p[:, 128 * t:128 * t + 128]
            spread = jnp.broadcast_to(chunk, (128, 128)).T
            for u in range(4):
                tile = gram_ref[128 * t:128 * t + 128, 128 * u:128 * u + 128] * spread
                parts[u] += jnp.sum(tile.reshape(16, 8, 128), axis=0)
        whole = jnp.concatenate([jnp.sum(v, axis=0, keepdims=True) for v in parts], axis=1)
        return whole * scale + lam_scaled * p

    def go_on(state):
        step, more = state[0], state[1]
        return jnp.logical_and(step < MAX_STEPS, more)

    def advance(state):
        step, _, s, r, p, v, old_rz, old_alpha = state
        more = (total(r * r) - bound * total(s * s))[0, 0] > 0.0
        u = r * jacobi
        rz = total(r * u)
        beta = rz / old_rz
        w = product(u)
        curve = total(w * u) - beta * rz / old_alpha
        good = curve > 0.0
        alpha = jnp.where(good, rz / curve, 0.0)
        p = u + beta * p
        v = w + beta * v
        old_rz = jnp.where(good, rz, jnp.inf)
        old_alpha = jnp.where(good, alpha, 1.0)
        return step + 1, more, s + alpha * p, r - alpha * v, p, v, old_rz, old_alpha

    r = cross_ref[0:1] / size
    zero = jnp.zeros_like(r)
    one = jnp.ones((1, 1), F32)
    state = (jnp.int32(0), jnp.bool_(True), zero, r, zero, zero, jnp.inf * one, one)
    s = lax.while_loop(go_on, advance, state)[2] * (size * scale)

    z = lax.rem(lax.axis_index("dp") // NC, NZ)
    for t in range(4):
        column[128 * t:128 * t + 128, :] = jnp.broadcast_to(s[:, 128 * t:128 * t + 128], (128, 128)).T
    for slot, o in enumerate(ORDER):
        at = pl.multiple_of(8 * lax.rem(z + (o + NZ), NZ), 8)
        for x in range(NX):
            ordered[pl.ds(128 * x + at, 8), :] = column[32 * slot + 8 * x:32 * slot + 8 * x + 8, :]
    for x in range(NX):
        out_ref[:, 128 * x:128 * x + 128] = ordered[128 * x:128 * x + 128, :].T[0:1, :]


def body(
    train_acts, train_grads, timestep, time_weight, query_acts, query_grads, proj_in, proj_out,
    damping,
):
    hbm = pl.BlockSpec(memory_space=pltpu.HBM)
    smem = pl.BlockSpec(memory_space=pltpu.SMEM)
    vmem = pl.BlockSpec(memory_space=pltpu.VMEM)
    dma = pltpu.SemaphoreType.DMA
    gram, cross = pl.pallas_call(
        gram_kernel,
        out_shape=(
            jax.ShapeDtypeStruct((512, 512), F32),
            jax.ShapeDtypeStruct((8, 512), F32),
        ),
        in_specs=[hbm] * 8,
        out_specs=(vmem, vmem),
        scratch_shapes=[
            pltpu.VMEM(train_acts.shape, BF),
            pltpu.VMEM(train_grads.shape, BF),
            pltpu.VMEM(query_acts.shape, BF),
            pltpu.VMEM(query_grads.shape, BF),
            pltpu.VMEM(proj_in.shape[::-1], BF),
            pltpu.VMEM(proj_out.shape[::-1], BF),
            pltpu.SMEM(timestep.shape, jnp.int32),
            pltpu.SMEM(time_weight.shape, F32),
            pltpu.VMEM((128, 128), F32),
            pltpu.VMEM((8, 16, 128), BF),
            pltpu.VMEM((8 * len(FAR), 16, 128), BF),
            pltpu.VMEM((128, 128), F32),
            pltpu.VMEM((4, 32, 128), F32),
            pltpu.VMEM((2, 8, 16, 256), BF),
            pltpu.VMEM((8, 16, 256), BF),
            pltpu.VMEM((8, 16, 256), BF),
            pltpu.VMEM((8, NZ, 32, 256), BF),
            pltpu.VMEM((256, 256), F32),
            pltpu.VMEM((272, 256), F32),
            pltpu.VMEM((272, 256), F32),
            pltpu.VMEM((256, 256), F32),
            pltpu.VMEM((272, 256), F32),
            pltpu.VMEM((272, 256), F32),
            dma((8,)),
            dma,
            dma((len(FAR),)),
            dma,
            dma((len(ORDER) - len(FAR),)),
            dma,
            dma((2,)),
            dma,
            dma,
            dma((3,)),
            dma((3,)),
        ],
        compiler_params=pltpu.CompilerParams(
            collective_id=0, has_side_effects=True, vmem_limit_bytes=40 << 20
        ),
        name="gather_gram",
    )(
        *[
            pltpu.with_memory_space_constraint(operand, pltpu.HBM)
            for operand in (
                train_acts, train_grads, timestep, time_weight, query_acts, query_grads,
                proj_in.T, proj_out.T,
            )
        ]
    )
    return pl.pallas_call(
        solve_kernel,
        out_shape=jax.ShapeDtypeStruct((1, 512), F32),
        in_specs=[vmem, vmem, smem],
        out_specs=vmem,
        scratch_shapes=[pltpu.VMEM((512, 128), F32)] * 2,
        compiler_params=pltpu.CompilerParams(vmem_limit_bytes=16 << 20),
        name="solve",
    )(gram, cross, damping)


def solution(mesh):
    return jax.shard_map(
        body,
        mesh=mesh,
        in_specs=(
            P("dp", None, None),
            P("dp", None, None),
            P("dp"),
            P(),
            P(("dp", "query"), None, None),
            P(("dp", "query"), None, None),
            P(),
            P(),
            P(),
        ),
        out_specs=P(("dp", "query"), None),
        check_vma=False,
    )
```
